32 devices in a mesh: bx: 8 (over z, y), by: 4 (over x, core).
Axes of the slice: x: 2, y: 2, z: 4, core: 2. Of those that a mesh axis runs over, the one named last changes fastest.
Arguments:
- tracer: float32 [24, 1024, 512], P(None, 'bx', 'by'), may hold values from -6 to 6
- velocity: float32 [2, 24, 1024, 512], P(None, None, 'bx', 'by'), may hold values from -6 to 6
- vert_diff: float32 [24, 1024, 512], P(None, 'bx', 'by'), may hold values from 0.05 to 5
- vert_visc: float32 [24, 1024, 512], P(None, 'bx', 'by'), may hold values from 0.05 to 5
- surface_flux: float32 [1024, 512], P('bx', 'by'), may hold values from -6 to 6
- wind_stress: float32 [2, 1024, 512], P(None, 'bx', 'by'), may hold values from -6 to 6
- surface_coef: float32 [1024, 512], P('bx', 'by'), may hold values from 0.3 to 3
- height: float32 [4, 48, 16, 128], P('by', 'bx'), may hold values from -6 to 6
- block_land: int32 [64, 4], replicated, may hold values from 0 to 1, as said below
- tropic_position_table: int32 [64, 4], replicated, may hold values from -1 to 47, as said below
Outputs:
- tracer_new: float32 [24, 1024, 512], P(None, 'bx', 'by')
- velocity_new: float32 [2, 24, 1024, 512], P(None, None, 'bx', 'by')
- fresh_height: float32 [4, 48, 16, 128], P('by', 'bx')
The draws below stay inside these ranges and needn't reach their ends.
Inputs may be any that keep to these rules, and one draw needn't show every extreme that they name: `block_land`: in each latitude row exactly 8 * (2) blocks are land. `tropic_position_table`: land blocks have -1; in each latitude row the ocean blocks hold the positions 0 to 47, each once, position p being slot p % 6 of longitude device p // 6. The ocean blocks that one longitude device holds in one row (blocks d * 8 to d * 8 + 7) go to different tropic devices.
All inputs are finite; a program needn't handle non-finite values.
Results may differ from the reference program's by a relative error of at most 0.000084.
Values sent between devices are 32-bit elements; how exact they have to be, the bound alone decides.
A program may use at most 128 MiB of HBM per device.

```python
import math
import jax
import jax.numpy as jnp

KZ = 24
DEVICE_LAT_CELLS = 128
BPD = 8
SLOTS = 6
ITERS = 4
BLOCK_LON_CELLS = 16
NX = 1024
NY = 512
NBX = 64
OCEAN_SLOT_COUNT = 48
N_BX = 8
N_BY = 4


def block_layout(key):

    def single_row(row):
        row_key = jax.random.fold_in(key, row)
        first_key, second_key, third_key = jax.random.split(row_key, 3)
        device_order = jax.random.permutation(first_key, N_BX)
        offsets = jax.random.permutation(second_key, N_BX)[:BPD]
        target = (device_order[:, None] + offsets[None, :]) % N_BX
        ranks = jax.vmap(lambda k: jax.random.permutation(k, BPD))(jax.random.split(third_key, N_BX))
        land_flag = (ranks < BPD - SLOTS).astype(jnp.int32)
        slot_of = jnp.cumsum(1 - land_flag, axis=1) - 1
        columns = jnp.broadcast_to(jnp.arange(BPD)[None, :], (N_BX, BPD))
        is_land = land_flag[target, columns]
        position = jnp.where(is_land == 1, -1, target * SLOTS + slot_of[target, columns])
        return (is_land.reshape(N_BX * BPD), position.reshape(N_BX * BPD))
    land_rows, position_rows = jax.vmap(single_row)(jnp.arange(N_BY))
    return (land_rows.T.astype(jnp.int32), position_rows.T.astype(jnp.int32))


def draw_block_land(key, part):
    land, position = block_layout(key)
    return land


def draw_tropic_position_table(key, part):
    land, position = block_layout(key)
    return position


def block_levels(stream_key, extent, pieces, low, high):
    level = 1.0
    for axis_at, shards_of in pieces:
        heights = jax.random.uniform(jax.random.fold_in(jax.random.fold_in(stream_key, 6), axis_at), (shards_of,), jnp.float32, low / len(pieces), high / len(pieces))
        level = level * jnp.repeat(jnp.exp(heights), extent[axis_at] // shards_of).reshape((-1,) + (1,) * (len(extent) - 1 - axis_at))
    return level


def scatter_about(key, dims, spread, reach, cuts=(), kind=jnp.bfloat16):
    level = block_levels(key, dims, cuts, -0.22, 0.18) if cuts else 1.0
    entries = jax.random.normal(key, dims, jnp.float32) * spread * level
    return jnp.minimum(jnp.maximum(entries, -reach), reach).astype(kind)


def setup_inputs(seed: int = 0) -> dict:
    key_of = jax.random.split(jax.random.key(seed), 11)
    tracer = scatter_about(key_of[0], (KZ, NX, NY), 1.0, 6.0, ((1, 8), (2, 4)), jnp.float32)
    velocity = scatter_about(key_of[1], (2, KZ, NX, NY), 1.0, 6.0, ((2, 8), (3, 4)), jnp.float32)
    vert_diff = jnp.clip(jnp.exp(math.log(5.0) - 4.6051702 * jax.random.uniform(key_of[2], (KZ, NX, NY), jnp.float32) ** block_levels(key_of[2], (KZ, NX, NY), ((1, 8), (2, 4)), -0.2, 0.2)), 0.05, 5.0)
    vert_visc = jnp.clip(jnp.exp(math.log(5.0) - 4.6051702 * jax.random.uniform(key_of[3], (KZ, NX, NY), jnp.float32) ** block_levels(key_of[3], (KZ, NX, NY), ((1, 8), (2, 4)), -0.2, 0.2)), 0.05, 5.0)
    surface_flux = scatter_about(key_of[4], (NX, NY), 1.0, 6.0, ((0, 8), (1, 4)), jnp.float32)
    wind_stress = scatter_about(key_of[5], (2, NX, NY), 1.0, 6.0, ((1, 8), (2, 4)), jnp.float32)
    surface_coef = jnp.clip(jnp.exp(math.log(3.0) - 2.3025851 * jax.random.uniform(key_of[6], (NX, NY), jnp.float32) ** block_levels(key_of[6], (NX, NY), ((0, 8), (1, 4)), -0.2, 0.2)), 0.3, 3.0)
    height = scatter_about(key_of[7], (N_BY, OCEAN_SLOT_COUNT, BLOCK_LON_CELLS, DEVICE_LAT_CELLS), 1.0, 6.0, ((0, 4), (1, 8)), jnp.float32)
    block_land = draw_block_land(jax.random.fold_in(key_of[10], 71), 0)
    tropic_position_table = draw_tropic_position_table(jax.random.fold_in(key_of[10], 71), 0)
    return dict(tracer=tracer, velocity=velocity, vert_diff=vert_diff, vert_visc=vert_visc, surface_flux=surface_flux, wind_stress=wind_stress, surface_coef=surface_coef, height=height, block_land=block_land, tropic_position_table=tropic_position_table)


MIX_RATE = 0.2
DIV_SCALE = 0.1
GRAVITY_STEP = 0.5
SIDE_WEIGHT = 1.0
CORNER_WEIGHT = 0.5
LOW_BOUND = 0.04
HIGH_BOUND = 2.0


def neighbour(field, step_x, step_y):
    moved = jnp.roll(field, -step_x, axis=-2)
    if step_y == 1:
        moved = jnp.concatenate([moved[..., 1:], jnp.zeros_like(moved[..., :1])], axis=-1)
    elif step_y == -1:
        moved = jnp.concatenate([jnp.zeros_like(moved[..., :1]), moved[..., :-1]], axis=-1)
    return moved


def vertical_solve(rhs, coef, thickness):
    levels = rhs.shape[1]
    ratios = []
    values = []
    for level in range(levels):
        if level < levels - 1:
            upper = coef[:, level] / thickness[level]
        else:
            upper = jnp.zeros_like(rhs[:, level])
        if level > 0:
            lower = coef[:, level - 1] / thickness[level]
        else:
            lower = jnp.zeros_like(rhs[:, level])
        centre = 1.0 + upper + lower
        if level == 0:
            denom = centre
            value = rhs[:, level] / denom
        else:
            denom = centre + lower * ratios[-1]
            value = (rhs[:, level] + lower * values[-1]) / denom
        ratios.append(-upper / denom)
        values.append(value)
    answer = [values[-1]]
    for level in range(levels - 2, -1, -1):
        answer.append(values[level] - ratios[level] * answer[-1])
    return jnp.stack(answer[::-1], axis=1)


def chebyshev(start, source, diagonal, operator):
    scale_a = 2.0 / (HIGH_BOUND - LOW_BOUND)
    gamma = (HIGH_BOUND + LOW_BOUND) / 2.0
    result = start
    residual = source - operator(result)
    update = residual / (gamma * diagonal)
    result = result + update
    weight = 2.0 / gamma
    for step in range(1, ITERS):
        residual = source - operator(result)
        weight = 1.0 / (gamma - weight / (4.0 * scale_a * scale_a))
        update = weight * residual / diagonal + (gamma * weight - 1.0) * update
        result = result + update
    return result


def reference(tracer, velocity, vert_diff, vert_visc, surface_flux, wind_stress, surface_coef, height, block_land, tropic_position_table):
    ocean_blocks = (1 - block_land).astype(jnp.float32)
    cells = jnp.repeat(jnp.repeat(ocean_blocks, BLOCK_LON_CELLS, axis=0), DEVICE_LAT_CELLS, axis=1)
    thickness = 1.0 + jnp.arange(KZ, dtype=jnp.float32) / KZ
    fields = jnp.concatenate([tracer[None], velocity], axis=0)
    total = jnp.zeros_like(fields)
    for step_x, step_y in ((1, 0), (-1, 0), (0, 1), (0, -1)):
        total = total + neighbour(cells, step_x, step_y) * (neighbour(fields, step_x, step_y) - fields)
    mixed = fields + MIX_RATE * (cells * total)
    rhs = mixed.at[:, 0].add(jnp.concatenate([surface_flux[None], wind_stress], axis=0) / thickness[0])
    coef = jnp.stack([vert_diff, vert_visc, vert_visc])
    solved = vertical_solve(rhs, coef, thickness) * cells
    transport = jnp.sum(thickness[:, None, None] * velocity, axis=1) * cells
    divergence = cells * (0.5 * ((neighbour(transport[0], 1, 0) - neighbour(transport[0], -1, 0))
                                 + (neighbour(transport[1], 0, 1) - neighbour(transport[1], 0, -1))))
    row_ids = jnp.broadcast_to(jnp.arange(N_BY, dtype=jnp.int32)[None, :], (NBX, N_BY))
    safe_ids = jnp.maximum(tropic_position_table, 0).astype(jnp.int32)
    old_blocks = height[row_ids, safe_ids] * ocean_blocks[:, :, None, None]
    start = cells * old_blocks.transpose(0, 2, 1, 3).reshape(NX, NY)
    source = cells * surface_coef * start - DIV_SCALE * divergence
    diagonal = surface_coef + 6.0

    def operator(field):
        sides = (neighbour(field, 1, 0) + neighbour(field, -1, 0)) + (neighbour(field, 0, 1) + neighbour(field, 0, -1))
        corners = (neighbour(field, 1, 1) + neighbour(field, -1, 1)) + (neighbour(field, 1, -1) + neighbour(field, -1, -1))
        return cells * (diagonal * field - SIDE_WEIGHT * sides - CORNER_WEIGHT * corners)

    surface = chebyshev(start, source, diagonal, operator)
    grad_x = 0.5 * (neighbour(surface, 1, 0) - neighbour(surface, -1, 0))
    grad_y = 0.5 * (neighbour(surface, 0, 1) - neighbour(surface, 0, -1))
    velocity_new = cells * (solved[1:] - GRAVITY_STEP * jnp.stack([grad_x, grad_y])[:, None])
    tracer_new = solved[0]
    new_blocks = surface.reshape(NBX, BLOCK_LON_CELLS, N_BY, DEVICE_LAT_CELLS).transpose(0, 2, 1, 3)
    placement_index = jnp.where(tropic_position_table < 0, OCEAN_SLOT_COUNT, tropic_position_table).astype(jnp.int32)
    fresh_height = jnp.zeros_like(height).at[row_ids, placement_index].set(new_blocks, mode="drop")
    return tracer_new, velocity_new, fresh_height
```

```python
import functools

import jax
import jax.numpy as jnp
from jax import lax
from jax.experimental import pallas as pl
from jax.experimental.pallas import tpu as pltpu
from jax.sharding import PartitionSpec as P

ITERS = 4
MIX_RATE = 0.2
DIV_SCALE = 0.1
GRAVITY_STEP = 0.5
LOW_BOUND = 0.04
HIGH_BOUND = 2.0

RIM = 8
CHUNK = 32
MESH = pl.DeviceIdType.MESH


def shift(value, step, axis):
    return pltpu.roll(value, (-step) % value.shape[axis], axis)


def kernel(
    counts,
    tracer,
    velocity,
    vert_diff,
    vert_visc,
    flux,
    wind,
    surface_coef,
    height,
    land,
    table,
    tracer_out,
    velocity_out,
    height_out,
    fields,
    diff,
    visc,
    solved_t,
    solved_v,
    ocean,
    weights,
    trans,
    packed,
    halo_p,
    row_send,
    row_recv,
    col_send,
    col_recv,
    start,
    halo_s,
    blocks_send,
    blocks_recv,
    fresh_send,
    fresh_recv,
    surface,
    grad,
    ratio,
    value,
    load_sem,
    out_sem,
    send_sem,
    recv_sem,
):
    n_x, n_y = counts
    levels, width_x, width_y = diff.shape
    slots, block_len = height.shape[1], height.shape[2]
    blocks = width_x // block_len
    total_blocks = land.shape[0]
    full_x = width_x + 2 * RIM
    top = RIM + width_x
    d = lax.axis_index("bx")
    r = lax.axis_index("by")
    east, west = lax.rem(d + 1, n_x), lax.rem(d + n_x - 1, n_x)
    north, south = lax.rem(r + 1, n_y), lax.rem(r + n_y - 1, n_y)
    thickness = [1.0 + k / levels for k in range(levels)]

    loads = []

    def load(src, dst):
        copy = pltpu.make_async_copy(src, dst, load_sem.at[len(loads)])
        copy.start()
        loads.append(copy)
        return copy

    rows = pl.ds(RIM, width_x)
    load_v = [
        load(velocity.at[c], fields.at[pl.ds((1 + c) * levels, levels), rows, :]) for c in range(2)
    ]
    load_t = load(tracer, fields.at[pl.ds(0, levels), rows, :])
    load_diff = load(vert_diff, diff)
    load_visc = load(vert_visc, visc)

    barrier = pltpu.get_barrier_semaphore()
    peers = [(lax.rem(d + step, n_x), r) for step in range(1, n_x)]
    peers += [(x, y) for y in (north, south) for x in (west, d, east)]
    for peer in peers:
        pl.semaphore_signal(barrier, inc=1, device_id=peer, device_id_type=MESH)

    sends = []

    def send(src, dst, peer):
        at = len(sends)
        copy = pltpu.make_async_remote_copy(
            src_ref=src,
            dst_ref=dst,
            send_sem=send_sem.at[at],
            recv_sem=recv_sem.at[at],
            device_id=peer,
            device_id_type=MESH,
        )
        copy.start()
        sends.append(copy)
        return copy

    slot_for = []
    for t in range(n_x):
        found = jnp.int32(-1)
        for j in range(blocks):
            off = table[t * blocks + j, r] - d * slots
            found = jnp.where((off >= 0) & (off < slots), off, found)
        slot_for.append(found)
        block = height[0, jnp.maximum(found, 0)]
        blocks_send[t] = jnp.where(found >= 0, block, 0.0)
    own_pos = [table[d * blocks + j, r] for j in range(blocks)]
    holder = [lax.div(jnp.maximum(pos, 0), jnp.int32(slots)) for pos in own_pos]

    lane = lax.broadcasted_iota(jnp.int32, (block_len, width_y), 1)
    row_north, row_south = jnp.minimum(r + 1, n_y - 1), jnp.maximum(r - 1, 0)
    for b in range(-1, blocks + 1):
        block_id = lax.rem(d * blocks + b + total_blocks, total_blocks)
        here = 1 - land[block_id, r]
        up = jnp.where(r < n_y - 1, 1 - land[block_id, row_north], 0)
        down = jnp.where(r > 0, 1 - land[block_id, row_south], 0)
        size = block_len if 0 <= b < blocks else RIM
        first = 0 if b < 0 else RIM + b * block_len
        at = pl.ds(first, size)
        ocean[at, :width_y] = jnp.full((size, width_y), here).astype(jnp.float32)
        ocean[at, width_y:] = jnp.where(lane[:size] < width_y // 2, up, down).astype(jnp.float32)

    pl.semaphore_wait(barrier, len(peers))
    a2a = [
        send(blocks_send.at[peers[i][0]], blocks_recv.at[d], peers[i]) for i in range(n_x - 1)
    ]
    blocks_recv[d] = blocks_send[d]

    for copy in load_v:
        copy.wait()
    for c in range(2):

        def add(k, total, c=c):
            scale = 1.0 + k.astype(jnp.float32) / levels
            return total + scale * fields[(1 + c) * levels + k, pl.ds(RIM, width_x), :]

        trans[c, pl.ds(RIM, width_x), :width_y] = lax.fori_loop(
            0, levels, add, jnp.zeros((width_x, width_y), jnp.float32), unroll=4
        )
    trans[2, pl.ds(RIM, width_x), :width_y] = surface_coef[...]
    wide = lax.broadcasted_iota(jnp.int32, (width_x, width_y), 1)
    half = width_y // 2
    t0 = trans[0, pl.ds(RIM, width_x), :width_y]
    t1 = trans[1, pl.ds(RIM, width_x), :width_y]
    t2 = surface_coef[...]
    low = jnp.where(
        wide < RIM, t0, jnp.where(wide < 2 * RIM, shift(t1, -RIM, 1), shift(t2, -2 * RIM, 1))
    )
    high = jnp.where(
        wide >= width_y - RIM,
        t0,
        jnp.where(wide >= width_y - 2 * RIM, shift(t1, RIM, 1), shift(t2, 2 * RIM, 1)),
    )
    packed[...] = jnp.where(wide < half, low, high)

    def halo(source_at, side_at, target, corners):
        out = []
        for to, peer_y in ((1, north), (0, south)):
            out.append(send(side_at(0, width_x), target.at[to, pl.ds(RIM, width_x), :], (d, peer_y)))
            out.append(
                send(side_at(width_x - RIM, RIM), target.at[to, pl.ds(0, RIM), :], (east, peer_y))
            )
            out.append(send(side_at(0, RIM), target.at[to, pl.ds(top, RIM), :], (west, peer_y)))
        out.append(send(source_at(width_x), corners(0), (east, d_row)))
        out.append(send(source_at(RIM), corners(top), (west, d_row)))
        return out

    d_row = r
    halo_trans = halo(
        lambda first: trans.at[:, pl.ds(first, RIM), pl.ds(0, width_y)],
        lambda first, size: packed.at[pl.ds(first, size), :],
        halo_p,
        lambda first: trans.at[:, pl.ds(first, RIM), pl.ds(0, width_y)],
    )

    load_t.wait()
    row_send[0] = fields[:, RIM, :]
    row_send[1] = fields[:, top - 1, :]
    row_copies = [
        send(row_send.at[1], row_recv.at[0], (east, r)),
        send(row_send.at[0], row_recv.at[1], (west, r)),
    ]
    lane_c = lax.broadcasted_iota(jnp.int32, (CHUNK, width_y), 1)

    def pack(i, carry):
        first = pl.multiple_of(i * CHUNK, CHUNK)
        low_cols = jnp.zeros((CHUNK, width_y), jnp.float32)
        high_cols = jnp.zeros((CHUNK, width_y), jnp.float32)
        for k in range(3 * levels):
            block = fields[k, pl.ds(first + RIM, CHUNK), :]
            low_cols = jnp.where(lane_c == k, block[:, :1], low_cols)
            high_cols = jnp.where(lane_c == k, block[:, width_y - 1 :], high_cols)
        col_send[0, pl.ds(first, CHUNK), :] = low_cols
        col_send[1, pl.ds(first, CHUNK), :] = high_cols
        return carry

    lax.fori_loop(0, width_x // CHUNK, pack, 0)
    col_copies = [
        send(col_send.at[1], col_recv.at[0], (d, north)),
        send(col_send.at[0], col_recv.at[1], (d, south)),
    ]

    for copy in a2a:
        copy.wait_recv()
    for j in range(blocks):
        at = pl.ds(RIM + j * block_len, block_len)
        start[at, :width_y] = ocean[at, :width_y] * blocks_recv[holder[j]]
    halo_start = halo(
        lambda first: start.at[pl.ds(first, RIM), pl.ds(0, width_y)],
        lambda first, size: start.at[pl.ds(RIM + first, size), pl.ds(0, width_y)],
        halo_s,
        lambda first: start.at[pl.ds(first, RIM), pl.ds(0, width_y)],
    )

    rim = ocean[...]
    inner = lambda padded: padded[RIM:top, :width_y]
    centre = inner(rim)
    total = jnp.zeros_like(centre)
    for at, (step, axis) in enumerate(((1, 0), (-1, 0), (1, 1), (-1, 1))):
        weight = MIX_RATE * (centre * inner(shift(rim, step, axis)))
        weights[1 + at] = weight
        total = total + weight
    weights[0] = 1.0 - total

    for copy in row_copies + col_copies:
        copy.wait_recv()
    fields[:, RIM - 1, :] = row_recv[0]
    fields[:, top, :] = row_recv[1]

    def columns(first_field, count, coef_ref, forcing, out_ref, final):
        def body(i, carry):
            first = pl.multiple_of(i * CHUNK, CHUNK)
            at = pl.ds(first, CHUNK)
            w0, w_e, w_w, w_n, w_s = [weights[n, at, :] for n in range(5)]
            below = col_recv[0, at, :]
            above = col_recv[1, at, :]
            gain = None
            last = [None] * count
            coef_up = None
            for k in range(levels):
                inv_thick = 1.0 / thickness[k]
                if k < levels - 1:
                    coef = coef_ref[k, at, :]
                    upper = coef * inv_thick
                if k > 0:
                    lower = coef_up * inv_thick
                if k == 0:
                    denom = 1.0 + upper
                elif k < levels - 1:
                    denom = (1.0 + upper) + lower * (1.0 - gain)
                else:
                    denom = 1.0 + lower * (1.0 - gain)
                inverse = 1.0 / denom
                if k < levels - 1:
                    gain = upper * inverse
                    ratio[k] = gain
                    coef_up = coef
                for f in range(count):
                    n = (first_field + f) * levels + k
                    block = fields[n, pl.ds(first, CHUNK + 2 * RIM), :]
                    mid = block[RIM : RIM + CHUNK]
                    near_n = jnp.where(
                        lane_c == width_y - 1, above[:, n : n + 1], shift(mid, 1, 1)
                    )
                    near_s = jnp.where(lane_c == 0, below[:, n : n + 1], shift(mid, -1, 1))
                    rhs = (
                        w0 * mid
                        + w_e * block[RIM + 1 : RIM + 1 + CHUNK]
                        + w_w * block[RIM - 1 : RIM - 1 + CHUNK]
                        + (w_n * near_n + w_s * near_s)
                    )
                    if k == 0:
                        rhs = rhs + forcing(f, at) / thickness[0]
                    else:
                        rhs = rhs + lower * last[f]
                    last[f] = rhs * inverse
                    if k < levels - 1:
                        value[f, k] = last[f]
            mask = ocean[pl.ds(first + RIM, CHUNK), :width_y]
            for k in range(levels - 1, -1, -1):
                for f in range(count):
                    if k < levels - 1:
                        last[f] = value[f, k] + ratio[k] * last[f]
                    out_ref[f * levels + k, at, :] = final(f, mask * last[f], at)
            return carry

        lax.fori_loop(0, width_x // CHUNK, body, 0)

    load_diff.wait()
    columns(0, 1, diff, lambda f, at: flux[at, :], solved_t, lambda f, x, at: x)
    out_t = pltpu.make_async_copy(solved_t, tracer_out, out_sem.at[0])
    out_t.start()

    for copy in halo_trans + halo_start:
        copy.wait_recv()
    full = lax.broadcasted_iota(jnp.int32, (full_x, width_y), 1)
    from_n, from_s = halo_p[0], halo_p[1]
    trans[0, :, width_y:] = jnp.where(full < half, from_n, from_s)
    trans[1, :, width_y:] = jnp.where(full < half, shift(from_n, RIM, 1), shift(from_s, -RIM, 1))
    trans[2, :, width_y:] = jnp.where(
        full < RIM,
        shift(from_n, 2 * RIM, 1),
        jnp.where(full >= width_y - RIM, shift(from_s, -2 * RIM, 1), 1.0),
    )
    start[:, width_y:] = ocean[:, width_y:] * jnp.where(full < half, halo_s[0], halo_s[1])
    wet = ocean[...]
    t0 = wet * trans[0]
    t1 = wet * trans[1]
    coef = trans[2]
    divergence = wet * (
        0.5 * ((shift(t0, 1, 0) - shift(t0, -1, 0)) + (shift(t1, 1, 1) - shift(t1, -1, 1)))
    )
    result = wet * start[...]
    source = wet * coef * result - DIV_SCALE * divergence
    diagonal = coef + 6.0
    inverse = 1.0 / diagonal

    def residual_of(field):
        pair = shift(field, 1, 0) + shift(field, -1, 0)
        mixed = field + 0.5 * pair
        near = pair + (shift(mixed, 1, 1) + shift(mixed, -1, 1))
        return source - wet * (diagonal * field - near)

    scale_a = 2.0 / (HIGH_BOUND - LOW_BOUND)
    gamma = (HIGH_BOUND + LOW_BOUND) / 2.0
    update = residual_of(result) * inverse * (1.0 / gamma)
    result = result + update
    weight = 2.0 / gamma
    for step in range(1, ITERS):
        weight = 1.0 / (gamma - weight / (4.0 * scale_a * scale_a))
        update = weight * (residual_of(result) * inverse) + (gamma * weight - 1.0) * update
        result = result + update
    for j in range(blocks):
        first = RIM + j * block_len
        surface[j] = result[first : first + block_len, :width_y]
    for t in range(n_x):
        found = jnp.int32(-1)
        for j in range(blocks):
            found = jnp.where((holder[j] == t) & (own_pos[j] >= 0), jnp.int32(j), found)
        fresh_send[t] = surface[jnp.maximum(found, 0)]
    fresh = [send(fresh_send.at[peers[i][0]], fresh_recv.at[d], peers[i]) for i in range(n_x - 1)]
    fresh_recv[d] = fresh_send[d]
    step_scale = GRAVITY_STEP * 0.5
    grad[0] = inner(wet * (step_scale * (shift(result, 1, 0) - shift(result, -1, 0))))
    grad[1] = inner(wet * (step_scale * (shift(result, 1, 1) - shift(result, -1, 1))))

    load_visc.wait()
    columns(
        1, 2, visc, lambda f, at: wind[f, at, :], solved_v, lambda f, x, at: x - grad[f, at, :]
    )
    out_v = [
        pltpu.make_async_copy(
            solved_v.at[pl.ds(c * levels, levels)], velocity_out.at[c], out_sem.at[1 + c]
        )
        for c in range(2)
    ]
    for copy in out_v:
        copy.start()

    for copy in fresh:
        copy.wait_recv()
    for s in range(slots):
        source_at = jnp.int32(0)
        for t in range(n_x):
            source_at = jnp.where(slot_for[t] == s, jnp.int32(t), source_at)
        height_out[0, s] = fresh_recv[source_at]
    for copy in sends:
        copy.wait_send()
    for copy in [out_t] + out_v:
        copy.wait()


def shards(counts, *args):
    tracer, velocity, height = args[0], args[1], args[7]
    levels, width_x, width_y = tracer.shape
    slots, block_len = height.shape[1], height.shape[2]
    blocks = width_x // block_len
    n_x, n_y = counts
    full_x = width_x + 2 * RIM
    n_sends = 2 * (n_x - 1) + 2 * 8 + 4
    f32 = jnp.float32
    vmem = pl.BlockSpec(memory_space=pltpu.VMEM)
    smem = pl.BlockSpec(memory_space=pltpu.SMEM)
    hbm = pl.BlockSpec(memory_space=pl.ANY)
    scratch = [
        pltpu.VMEM((3 * levels, full_x, width_y), f32),
        pltpu.VMEM((levels, width_x, width_y), f32),
        pltpu.VMEM((levels, width_x, width_y), f32),
        pltpu.VMEM((levels, width_x, width_y), f32),
        pltpu.VMEM((2 * levels, width_x, width_y), f32),
        pltpu.VMEM((full_x, 2 * width_y), f32),
        pltpu.VMEM((5, width_x, width_y), f32),
        pltpu.VMEM((3, full_x, 2 * width_y), f32),
        pltpu.VMEM((width_x, width_y), f32),
        pltpu.VMEM((2, full_x, width_y), f32),
        pltpu.VMEM((2, 3 * levels, width_y), f32),
        pltpu.VMEM((2, 3 * levels, width_y), f32),
        pltpu.VMEM((2, width_x, width_y), f32),
        pltpu.VMEM((2, width_x, width_y), f32),
        pltpu.VMEM((full_x, 2 * width_y), f32),
        pltpu.VMEM((2, full_x, width_y), f32),
        pltpu.VMEM((n_x, block_len, width_y), f32),
        pltpu.VMEM((n_x, block_len, width_y), f32),
        pltpu.VMEM((n_x, block_len, width_y), f32),
        pltpu.VMEM((n_x, block_len, width_y), f32),
        pltpu.VMEM((blocks, block_len, width_y), f32),
        pltpu.VMEM((2, width_x, width_y), f32),
        pltpu.VMEM((levels, CHUNK, width_y), f32),
        pltpu.VMEM((2, levels, CHUNK, width_y), f32),
        pltpu.SemaphoreType.DMA((5,)),
        pltpu.SemaphoreType.DMA((3,)),
        pltpu.SemaphoreType.DMA((n_sends,)),
        pltpu.SemaphoreType.DMA((n_sends,)),
    ]
    return pl.pallas_call(
        functools.partial(kernel, counts),
        out_shape=(
            jax.ShapeDtypeStruct(tracer.shape, f32),
            jax.ShapeDtypeStruct(velocity.shape, f32),
            jax.ShapeDtypeStruct(height.shape, f32),
        ),
        in_specs=[hbm, hbm, hbm, hbm, vmem, vmem, vmem, vmem, smem, smem],
        out_specs=(hbm, hbm, vmem),
        scratch_shapes=scratch,
        compiler_params=pltpu.CompilerParams(
            collective_id=0, has_side_effects=True, vmem_limit_bytes=40 * 1024 * 1024
        ),
        cost_estimate=pl.CostEstimate(
            flops=40 * 3 * levels * width_x * width_y,
            bytes_accessed=8 * 4 * levels * width_x * width_y,
            transcendentals=0,
        ),
    )(*args)


def solution(mesh):
    placed = (
        P(None, "bx", "by"),
        P(None, None, "bx", "by"),
        P(None, "bx", "by"),
        P(None, "bx", "by"),
        P("bx", "by"),
        P(None, "bx", "by"),
        P("bx", "by"),
        P("by", "bx", None, None),
        P(),
        P(),
    )
    return jax.shard_map(
        functools.partial(shards, (mesh.shape["bx"], mesh.shape["by"])),
        mesh=mesh,
        in_specs=placed,
        out_specs=(P(None, "bx", "by"), P(None, None, "bx", "by"), P("by", "bx", None, None)),
        check_vma=False,
    )
```

```python
import functools

import jax
import jax.numpy as jnp
from jax import lax
from jax.experimental import pallas as pl
from jax.experimental.pallas import tpu as pltpu
from jax.sharding import PartitionSpec as P

ITERS = 4
MIX_RATE = 0.2
DIV_SCALE = 0.1
GRAVITY_STEP = 0.5
LOW_BOUND = 0.04
HIGH_BOUND = 2.0

RIM = 8
CHUNK = 32
MESH = pl.DeviceIdType.MESH


def shift(value, step, axis):
    return pltpu.roll(value, (-step) % value.shape[axis], axis)


def kernel(
    counts,
    tracer,
    velocity,
    vert_diff,
    vert_visc,
    flux_in,
    wind_in,
    surface_coef_in,
    height_in,
    land,
    table,
    tracer_out,
    velocity_out,
    height_out,
    fields,
    diff,
    visc,
    solved_t,
    solved_v,
    flux,
    wind,
    surface_coef,
    height,
    ocean,
    weights,
    trans,
    packed,
    halo_p,
    row_send,
    row_recv,
    col_send,
    col_recv,
    start,
    halo_s,
    blocks_send,
    blocks_recv,
    fresh_send,
    fresh_recv,
    surface,
    grad,
    ratio,
    value,
    load_sem,
    out_sem,
    send_sem,
    recv_sem,
):
    n_x, n_y = counts
    levels, width_x, width_y = diff.shape
    slots, block_len = height.shape[1], height.shape[2]
    blocks = width_x // block_len
    total_blocks = land.shape[1]
    full_x = width_x + 2 * RIM
    top = RIM + width_x
    d = lax.axis_index("bx")
    r = lax.axis_index("by")
    east, west = lax.rem(d + 1, n_x), lax.rem(d + n_x - 1, n_x)
    north, south = lax.rem(r + 1, n_y), lax.rem(r + n_y - 1, n_y)
    thickness = [1.0 + k / levels for k in range(levels)]

    loads = []

    def load(src, dst):
        copy = pltpu.make_async_copy(src, dst, load_sem.at[len(loads)])
        copy.start()
        loads.append(copy)
        return copy

    rows = pl.ds(RIM, width_x)
    load_height = load(height_in, height)
    load_v = [
        load(velocity.at[c], fields.at[pl.ds((1 + c) * levels, levels), rows, :]) for c in range(2)
    ]
    load_coef = load(surface_coef_in, surface_coef)
    load_t = load(tracer, fields.at[pl.ds(0, levels), rows, :])
    load_diff = load(vert_diff, diff)
    load_flux = load(flux_in, flux)
    load_visc = load(vert_visc, visc)
    load_wind = load(wind_in, wind)

    barrier = pltpu.get_barrier_semaphore()
    peers = [(lax.rem(d + step, n_x), r) for step in range(1, n_x)]
    peers += [(x, y) for y in (north, south) for x in (west, d, east)]
    for peer in peers:
        pl.semaphore_signal(barrier, inc=1, device_id=peer, device_id_type=MESH)

    sends = []

    def send(src, dst, peer):
        at = len(sends)
        copy = pltpu.make_async_remote_copy(
            src_ref=src,
            dst_ref=dst,
            send_sem=send_sem.at[at],
            recv_sem=recv_sem.at[at],
            device_id=peer,
            device_id_type=MESH,
        )
        copy.start()
        sends.append(copy)
        return copy

    load_height.wait()
    slot_for = []
    for t in range(n_x):
        found = jnp.int32(-1)
        for j in range(blocks):
            off = table[r, t * blocks + j] - d * slots
            found = jnp.where((off >= 0) & (off < slots), off, found)
        slot_for.append(found)
        block = height[0, jnp.maximum(found, 0)]
        blocks_send[t] = jnp.where(found >= 0, block, 0.0)
    own_pos = [table[r, d * blocks + j] for j in range(blocks)]
    holder = [lax.div(jnp.maximum(pos, 0), jnp.int32(slots)) for pos in own_pos]

    lane = lax.broadcasted_iota(jnp.int32, (block_len, width_y), 1)
    row_north, row_south = jnp.minimum(r + 1, n_y - 1), jnp.maximum(r - 1, 0)
    for b in range(-1, blocks + 1):
        block_id = lax.rem(d * blocks + b + total_blocks, total_blocks)
        here = 1 - land[r, block_id]
        up = jnp.where(r < n_y - 1, 1 - land[row_north, block_id], 0)
        down = jnp.where(r > 0, 1 - land[row_south, block_id], 0)
        size = block_len if 0 <= b < blocks else RIM
        first = 0 if b < 0 else RIM + b * block_len
        at = pl.ds(first, size)
        ocean[at, :width_y] = jnp.full((size, width_y), here).astype(jnp.float32)
        ocean[at, width_y:] = jnp.where(lane[:size] < width_y // 2, up, down).astype(jnp.float32)

    pl.semaphore_wait(barrier, len(peers))
    a2a = [
        send(blocks_send.at[peers[i][0]], blocks_recv.at[d], peers[i]) for i in range(n_x - 1)
    ]
    blocks_recv[d] = blocks_send[d]

    for copy in load_v:
        copy.wait()
    for c in range(2):

        def add(k, total, c=c):
            scale = 1.0 + k.astype(jnp.float32) / levels
            return total + scale * fields[(1 + c) * levels + k, pl.ds(RIM, width_x), :]

        trans[c, pl.ds(RIM, width_x), :width_y] = lax.fori_loop(
            0, levels, add, jnp.zeros((width_x, width_y), jnp.float32), unroll=4
        )
    load_coef.wait()
    trans[2, pl.ds(RIM, width_x), :width_y] = surface_coef[...]
    wide = lax.broadcasted_iota(jnp.int32, (width_x, width_y), 1)
    half = width_y // 2
    t0 = trans[0, pl.ds(RIM, width_x), :width_y]
    t1 = trans[1, pl.ds(RIM, width_x), :width_y]
    t2 = surface_coef[...]
    low = jnp.where(
        wide < RIM, t0, jnp.where(wide < 2 * RIM, shift(t1, -RIM, 1), shift(t2, -2 * RIM, 1))
    )
    high = jnp.where(
        wide >= width_y - RIM,
        t0,
        jnp.where(wide >= width_y - 2 * RIM, shift(t1, RIM, 1), shift(t2, 2 * RIM, 1)),
    )
    packed[...] = jnp.where(wide < half, low, high)

    def halo(source_at, side_at, target, corners):
        out = []
        for to, peer_y in ((1, north), (0, south)):
            out.append(send(side_at(0, width_x), target.at[to, pl.ds(RIM, width_x), :], (d, peer_y)))
            out.append(
                send(side_at(width_x - RIM, RIM), target.at[to, pl.ds(0, RIM), :], (east, peer_y))
            )
            out.append(send(side_at(0, RIM), target.at[to, pl.ds(top, RIM), :], (west, peer_y)))
        out.append(send(source_at(width_x), corners(0), (east, d_row)))
        out.append(send(source_at(RIM), corners(top), (west, d_row)))
        return out

    d_row = r
    halo_trans = halo(
        lambda first: trans.at[:, pl.ds(first, RIM), pl.ds(0, width_y)],
        lambda first, size: packed.at[pl.ds(first, size), :],
        halo_p,
        lambda first: trans.at[:, pl.ds(first, RIM), pl.ds(0, width_y)],
    )

    load_t.wait()
    row_send[0] = fields[:, RIM, :]
    row_send[1] = fields[:, top - 1, :]
    row_copies = [
        send(row_send.at[1], row_recv.at[0], (east, r)),
        send(row_send.at[0], row_recv.at[1], (west, r)),
    ]
    lane_c = lax.broadcasted_iota(jnp.int32, (CHUNK, width_y), 1)

    def pack(i, carry):
        first = pl.multiple_of(i * CHUNK, CHUNK)
        low_cols = jnp.zeros((CHUNK, width_y), jnp.float32)
        high_cols = jnp.zeros((CHUNK, width_y), jnp.float32)
        for k in range(3 * levels):
            block = fields[k, pl.ds(first + RIM, CHUNK), :]
            turned = pltpu.roll(block, k, 1) if k else block
            low_cols = jnp.where(lane_c == k, turned, low_cols)
            high_cols = jnp.where(lane_c == (k - 1) % width_y, turned, high_cols)
        col_send[0, pl.ds(first, CHUNK), :] = low_cols
        col_send[1, pl.ds(first, CHUNK), :] = high_cols
        return carry

    lax.fori_loop(0, width_x // CHUNK, pack, 0)
    col_copies = [
        send(col_send.at[1], col_recv.at[0], (d, north)),
        send(col_send.at[0], col_recv.at[1], (d, south)),
    ]

    for copy in a2a:
        copy.wait_recv()
    for j in range(blocks):
        at = pl.ds(RIM + j * block_len, block_len)
        start[at, :width_y] = ocean[at, :width_y] * blocks_recv[holder[j]]
    halo_start = halo(
        lambda first: start.at[pl.ds(first, RIM), pl.ds(0, width_y)],
        lambda first, size: start.at[pl.ds(RIM + first, size), pl.ds(0, width_y)],
        halo_s,
        lambda first: start.at[pl.ds(first, RIM), pl.ds(0, width_y)],
    )

    rim = ocean[...]
    inner = lambda padded: padded[RIM:top, :width_y]
    centre = inner(rim)
    total = jnp.zeros_like(centre)
    for at, (step, axis) in enumerate(((1, 0), (-1, 0), (1, 1), (-1, 1))):
        weight = MIX_RATE * (centre * inner(shift(rim, step, axis)))
        weights[1 + at] = weight
        total = total + weight
    weights[0] = 1.0 - total

    for copy in row_copies + col_copies:
        copy.wait_recv()
    fields[:, RIM - 1, :] = row_recv[0]
    fields[:, top, :] = row_recv[1]

    def columns(first_field, count, coef_ref, forcing, store, after=None):
        def body(i, carry):
            first = pl.multiple_of(i * CHUNK, CHUNK)
            at = pl.ds(first, CHUNK)
            w0, w_e, w_w, w_n, w_s = [weights[n, at, :] for n in range(5)]
            below = col_recv[0, at, :]
            above = col_recv[1, at, :]
            gain = None
            last = [None] * count
            coef_up = None
            for k in range(levels):
                inv_thick = 1.0 / thickness[k]
                if k < levels - 1:
                    coef = coef_ref[k, at, :]
                    upper = coef * inv_thick
                if k > 0:
                    lower = coef_up * inv_thick
                if k == 0:
                    denom = 1.0 + upper
                elif k < levels - 1:
                    denom = (1.0 + upper) + lower * (1.0 - gain)
                else:
                    denom = 1.0 + lower * (1.0 - gain)
                inverse = 1.0 / denom
                if k < levels - 1:
                    gain = upper * inverse
                    ratio[k] = gain
                    coef_up = coef
                for f in range(count):
                    n = (first_field + f) * levels + k
                    block = fields[n, pl.ds(first, CHUNK + 2 * RIM), :]
                    mid = block[RIM : RIM + CHUNK]
                    near_n = jnp.where(
                        lane_c == width_y - 1, above[:, n : n + 1], shift(mid, 1, 1)
                    )
                    near_s = jnp.where(
                        lane_c == 0, below[:, (n - 1) % width_y][:, None], shift(mid, -1, 1)
                    )
                    rhs = (
                        w0 * mid
                        + w_e * block[RIM + 1 : RIM + 1 + CHUNK]
                        + w_w * block[RIM - 1 : RIM - 1 + CHUNK]
                        + (w_n * near_n + w_s * near_s)
                    )
                    if k == 0:
                        rhs = rhs + forcing(f, at) / thickness[0]
                    else:
                        rhs = rhs + lower * last[f]
                    last[f] = rhs * inverse
                    if k < levels - 1:
                        value[f, k] = last[f]
            mask = ocean[pl.ds(first + RIM, CHUNK), :width_y]
            for k in range(levels - 1, -1, -1):
                for f in range(count):
                    if k < levels - 1:
                        last[f] = value[f, k] + ratio[k] * last[f]
                    store(f, k, at, mask * last[f])
            return carry

        def step(i, carry):
            body(i, carry)
            if after is not None:
                after(i).start()
            return carry

        lax.fori_loop(0, width_x // CHUNK, step, 0)

    load_diff.wait()
    load_flux.wait()

    def store_t(f, k, at, x):
        solved_t[k, at, :] = x

    columns(0, 1, diff, lambda f, at: flux[at, :], store_t)
    out_t = pltpu.make_async_copy(solved_t, tracer_out, out_sem.at[width_x // CHUNK])
    out_t.start()

    for copy in halo_trans + halo_start:
        copy.wait_recv()
    full = lax.broadcasted_iota(jnp.int32, (full_x, width_y), 1)
    from_n, from_s = halo_p[0], halo_p[1]
    trans[0, :, width_y:] = jnp.where(full < half, from_n, from_s)
    trans[1, :, width_y:] = jnp.where(full < half, shift(from_n, RIM, 1), shift(from_s, -RIM, 1))
    trans[2, :, width_y:] = jnp.where(
        full < RIM,
        shift(from_n, 2 * RIM, 1),
        jnp.where(full >= width_y - RIM, shift(from_s, -2 * RIM, 1), 1.0),
    )
    start[:, width_y:] = ocean[:, width_y:] * jnp.where(full < half, halo_s[0], halo_s[1])
    wet = ocean[...]
    t0 = wet * trans[0]
    t1 = wet * trans[1]
    coef = trans[2]
    divergence = wet * (
        0.5 * ((shift(t0, 1, 0) - shift(t0, -1, 0)) + (shift(t1, 1, 1) - shift(t1, -1, 1)))
    )
    result = wet * start[...]
    source = wet * coef * result - DIV_SCALE * divergence
    diagonal = coef + 6.0
    inverse = 1.0 / diagonal

    def residual_of(field):
        pair = shift(field, 1, 0) + shift(field, -1, 0)
        mixed = field + 0.5 * pair
        near = pair + (shift(mixed, 1, 1) + shift(mixed, -1, 1))
        return source - wet * (diagonal * field - near)

    scale_a = 2.0 / (HIGH_BOUND - LOW_BOUND)
    gamma = (HIGH_BOUND + LOW_BOUND) / 2.0
    update = residual_of(result) * inverse * (1.0 / gamma)
    result = result + update
    weight = 2.0 / gamma
    for step in range(1, ITERS):
        weight = 1.0 / (gamma - weight / (4.0 * scale_a * scale_a))
        update = weight * (residual_of(result) * inverse) + (gamma * weight - 1.0) * update
        result = result + update
    for j in range(blocks):
        first = RIM + j * block_len
        surface[j] = result[first : first + block_len, :width_y]
    for t in range(n_x):
        found = jnp.int32(-1)
        for j in range(blocks):
            found = jnp.where((holder[j] == t) & (own_pos[j] >= 0), jnp.int32(j), found)
        fresh_send[t] = surface[jnp.maximum(found, 0)]
    fresh = [send(fresh_send.at[peers[i][0]], fresh_recv.at[d], peers[i]) for i in range(n_x - 1)]
    fresh_recv[d] = fresh_send[d]
    step_scale = GRAVITY_STEP * 0.5
    grad[0] = inner(wet * (step_scale * (shift(result, 1, 0) - shift(result, -1, 0))))
    grad[1] = inner(wet * (step_scale * (shift(result, 1, 1) - shift(result, -1, 1))))

    load_visc.wait()
    load_wind.wait()

    def store_v(f, k, at, x):
        solved_v[f, k, at, :] = x - grad[f, at, :]

    def out_v(i):
        at = pl.ds(pl.multiple_of(i * CHUNK, CHUNK), CHUNK)
        return pltpu.make_async_copy(
            solved_v.at[:, :, at, :], velocity_out.at[:, :, at, :], out_sem.at[i]
        )

    columns(1, 2, visc, lambda f, at: wind[f, at, :], store_v, out_v)

    for copy in fresh:
        copy.wait_recv()
    for s in range(slots):
        source_at = jnp.int32(0)
        for t in range(n_x):
            source_at = jnp.where(slot_for[t] == s, jnp.int32(t), source_at)
        height_out[0, s] = fresh_recv[source_at]
    for copy in sends:
        copy.wait_send()
    out_t.wait()
    for i in range(width_x // CHUNK):
        out_v(i).wait()


def write_out(a, b, c, a_out, b_out, c_out, a_held, b_held, c_held, in_sems, out_sems):
    pieces = [(c, c_held, c_out)]
    third = a.shape[0] // 3
    for i in range(3):
        at = pl.ds(i * third, third)
        pieces.append((a.at[at], a_held.at[at], a_out.at[at]))
        pieces += [(b.at[n, at], b_held.at[n, at], b_out.at[n, at]) for n in range(2)]
    reads = [pltpu.make_async_copy(x, h, in_sems.at[i]) for i, (x, h, _) in enumerate(pieces)]
    writes = [pltpu.make_async_copy(h, y, out_sems.at[i]) for i, (_, h, y) in enumerate(pieces)]
    for copy in reads:
        copy.start()
    for read, write in zip(reads, writes):
        read.wait()
        write.start()
    for copy in writes:
        copy.wait()


def shards(counts, *args):
    tracer, velocity, height = args[0], args[1], args[7]
    levels, width_x, width_y = tracer.shape
    slots, block_len = height.shape[1], height.shape[2]
    blocks = width_x // block_len
    n_x, n_y = counts
    full_x = width_x + 2 * RIM
    n_sends = 2 * (n_x - 1) + 2 * 8 + 4
    f32 = jnp.float32
    vmem = pl.BlockSpec(memory_space=pltpu.VMEM)
    smem = pl.BlockSpec(memory_space=pltpu.SMEM)
    hbm = pl.BlockSpec(memory_space=pltpu.HBM)
    scratch = [
        pltpu.VMEM((3 * levels, full_x, width_y), f32),
        pltpu.VMEM((levels, width_x, width_y), f32),
        pltpu.VMEM((levels, width_x, width_y), f32),
        pltpu.VMEM((levels, width_x, width_y), f32),
        pltpu.VMEM((2, levels, width_x, width_y), f32),
        pltpu.VMEM((width_x, width_y), f32),
        pltpu.VMEM((2, width_x, width_y), f32),
        pltpu.VMEM((width_x, width_y), f32),
        pltpu.VMEM(height.shape, f32),
        pltpu.VMEM((full_x, 2 * width_y), f32),
        pltpu.VMEM((5, width_x, width_y), f32),
        pltpu.VMEM((3, full_x, 2 * width_y), f32),
        pltpu.VMEM((width_x, width_y), f32),
        pltpu.VMEM((2, full_x, width_y), f32),
        pltpu.VMEM((2, 3 * levels, width_y), f32),
        pltpu.VMEM((2, 3 * levels, width_y), f32),
        pltpu.VMEM((2, width_x, width_y), f32),
        pltpu.VMEM((2, width_x, width_y), f32),
        pltpu.VMEM((full_x, 2 * width_y), f32),
        pltpu.VMEM((2, full_x, width_y), f32),
        pltpu.VMEM((n_x, block_len, width_y), f32),
        pltpu.VMEM((n_x, block_len, width_y), f32),
        pltpu.VMEM((n_x, block_len, width_y), f32),
        pltpu.VMEM((n_x, block_len, width_y), f32),
        pltpu.VMEM((blocks, block_len, width_y), f32),
        pltpu.VMEM((2, width_x, width_y), f32),
        pltpu.VMEM((levels, CHUNK, width_y), f32),
        pltpu.VMEM((2, levels, CHUNK, width_y), f32),
        pltpu.SemaphoreType.DMA((9,)),
        pltpu.SemaphoreType.DMA((1 + width_x // CHUNK,)),
        pltpu.SemaphoreType.DMA((n_sends,)),
        pltpu.SemaphoreType.DMA((n_sends,)),
    ]
    outs = pl.pallas_call(
        functools.partial(kernel, counts),
        out_shape=(
            jax.ShapeDtypeStruct(tracer.shape, f32),
            jax.ShapeDtypeStruct(velocity.shape, f32),
            jax.ShapeDtypeStruct(height.shape, f32),
        ),
        in_specs=[hbm] * 8 + [smem] * 2,
        out_specs=(hbm, hbm, vmem),
        scratch_shapes=scratch,
        compiler_params=pltpu.CompilerParams(
            collective_id=0, has_side_effects=True, vmem_limit_bytes=60 * 1024 * 1024
        ),
        cost_estimate=pl.CostEstimate(
            flops=40 * 3 * levels * width_x * width_y,
            bytes_accessed=8 * 4 * levels * width_x * width_y,
            transcendentals=0,
        ),
    )(*args[:8], args[8].T, args[9].T)
    return pl.pallas_call(
        write_out,
        out_shape=tuple(jax.ShapeDtypeStruct(out.shape, f32) for out in outs),
        in_specs=[hbm] * 3,
        out_specs=(hbm,) * 3,
        scratch_shapes=[pltpu.VMEM(out.shape, f32) for out in outs]
        + [pltpu.SemaphoreType.DMA((10,))] * 2,
        compiler_params=pltpu.CompilerParams(vmem_limit_bytes=60 * 1024 * 1024),
    )(*outs)


def solution(mesh):
    placed = (
        P(None, "bx", "by"),
        P(None, None, "bx", "by"),
        P(None, "bx", "by"),
        P(None, "bx", "by"),
        P("bx", "by"),
        P(None, "bx", "by"),
        P("bx", "by"),
        P("by", "bx", None, None),
        P(),
        P(),
    )
    return jax.shard_map(
        functools.partial(shards, (mesh.shape["bx"], mesh.shape["by"])),
        mesh=mesh,
        in_specs=placed,
        out_specs=(P(None, "bx", "by"), P(None, None, "bx", "by"), P("by", "bx", None, None)),
        check_vma=False,
    )
```
